32 devices in a mesh: grp: 8 (over y, x, core), rep: 4 (over z).
Axes of the slice: x: 2, y: 2, z: 4, core: 2. Of those that a mesh axis runs over, the one named last changes fastest.
Arguments:
- tokens: bfloat16 [32768, 768], P(('grp', 'rep')), may hold values from -6 to 6
- gain_attn: bfloat16 [768], P('grp'), may hold values from 0.5 to 1.5
- w_query: bfloat16 [768, 768], P('grp'), may hold values from -0.21875 to 0.21875
- w_key: bfloat16 [768, 768], P('grp'), may hold values from -0.21875 to 0.21875
- w_value: bfloat16 [768, 768], P('grp'), may hold values from -0.21875 to 0.21875
- w_out: bfloat16 [768, 768], P('grp'), may hold values from -3.5 to 3.5
- gain_ffn: bfloat16 [768], P('grp'), may hold values from 0.5 to 1.5
- w_router: bfloat16 [768, 8], P('grp'), may hold values from -0.14941406 to 0.14941406
- w_in: bfloat16 [8, 768, 3072], P('grp'), may hold values from -0.21875 to 0.21875
- w_expert_out: bfloat16 [8, 3072, 768], P('grp'), may hold values from -1.75 to 1.75
- bias_table: bfloat16 [32, 12], P('grp'), may hold values from -4 to 4
- bucket_ids: int32 [2047], replicated, may hold values from 0 to 31
- routes: int32 [32768, 1], P(('grp', 'rep')), may hold values from 0 to 7; in each aligned block of 1024 rows (0 to 1023, 1024 to 2047, ...) at most 192 rows name the same one
- cotangent: bfloat16 [32768, 768], P(('grp', 'rep')), may hold values from -6 to 6
Outputs:
- output: bfloat16 [32768, 768], P(('grp', 'rep'))
- input_grad: float32 [32768, 768], P(('grp', 'rep'))
- grad_gain_attn: float32 [768], P('grp')
- grad_query: float32 [768, 768], P('grp')
- grad_key: float32 [768, 768], P('grp')
- grad_value: float32 [768, 768], P('grp')
- grad_out: float32 [768, 768], P('grp')
- grad_gain_ffn: float32 [768], P('grp')
- grad_router: float32 [768, 8], P('grp')
- grad_expert_in: float32 [8, 768, 3072], P('grp')
- grad_expert_out: float32 [8, 3072, 768], P('grp')
- grad_table: float32 [32, 12], P('grp')
The draws below stay inside these ranges and needn't reach their ends.
Inputs may be any that keep to these rules, and one draw needn't show every extreme that they name: `routes`: in each device's aligned block of 1024 rows no expert is named more than 192 times, a bound that some block reaches.
All inputs are finite; a program needn't handle non-finite values.
Results may differ from the reference program's by a relative error of at most 0.02.
Values may be sent and summed in bfloat16 or wider, within the bound.
A program may use at most 384 MiB of HBM per device.

```python
import math
import jax
import jax.numpy as jnp
import numpy as np
from jax import lax

D = 768
HEADS = 12
HEAD_DIM = 64
FF = 3072
BUCKETS = 32
SEQ = 1024
SEQS_DEV = 1
TOK_DEV = 1024
EXPERTS = 8
CAP = 192
TOKENS = 32768


def place_ends(entries, key, least, high):
    shape = entries.shape
    spot = [jax.random.randint(jax.random.fold_in(key, axis), (), 0, shape[axis]) for axis in range(len(shape))]
    entries = entries.at[tuple(spot)].set(least)
    longest = shape.index(max(shape))
    spot[longest] = (spot[longest] + 1) % shape[longest]
    return entries.at[tuple(spot)].set(high)


def shard_levels(rng, shape, split, least, high):
    def one(dim, parts):
        draws = jax.random.uniform(jax.random.fold_in(jax.random.fold_in(rng, 6), dim), (parts,), jnp.float32, least / len(split), high / len(split))
        return jnp.repeat(jnp.exp(draws), shape[dim] // parts).reshape((-1,) + (1,) * (len(shape) - dim - 1))

    loudness = one(*split[0])
    for cut in split[1:]:
        loudness = loudness * one(*cut)
    return loudness


def shared_out(own_key, own, number, rows, amount, top, bound, slope):
    order = jax.random.permutation(own_key, amount)
    crowded, usual = load_shares(amount, rows * top, bound, slope, True), load_shares(amount, rows * top, bound, slope, False)
    places = jnp.arange(amount)

    def named(tallies, offset_by):
        used = int((tallies > 0).sum())
        fixed = max(1, used // 4)
        moved = fixed + (places - fixed + offset_by * (used - fixed)) % max(1, amount - fixed)
        return jnp.zeros((amount,), jnp.int32).at[order[jnp.where(places < fixed, places, moved)]].set(jnp.asarray(tallies, jnp.int32))

    tallies = jnp.where(number % 4 == 0, named(crowded, number // 4), named(usual, number - number // 4 - 1))
    mixed = jax.random.permutation(jax.random.fold_in(own, 3), amount)
    donor, sink = mixed[0:amount // 2 * 2:2], mixed[1:amount // 2 * 2:2]
    margin = jnp.minimum(tallies[donor] - 1, bound - tallies[sink]) // 2
    margin = jnp.where((donor == order[0]) | (sink == order[0]) | (tallies[sink] == 0), 0, jnp.maximum(margin, 0))
    moved = jax.random.randint(jax.random.fold_in(own, 4), (amount // 2,), 0, 1 << 20) % (margin + 1)
    tallies = tallies.at[donor].add(-moved).at[sink].add(moved)
    members = jnp.searchsorted(jnp.cumsum(tallies), jnp.arange(rows * top), side="right").astype(jnp.int32)
    grid = members.reshape(top, rows).T
    grid = grid[jax.random.permutation(jax.random.fold_in(own, 1), rows)]
    offset_by = jax.random.randint(jax.random.fold_in(own, 2), (rows, 1), 0, top)
    return jnp.take_along_axis(grid, (jnp.arange(top)[None, :] + offset_by) % top, axis=1)


def load_shares(number_of, total, limit, slope, full):
    loads = [(1 << 20) // math.isqrt(grade ** slope) + 1 for grade in range(1, number_of + 1)]
    largest = limit if full else min(limit, max(-(-total // number_of), total * loads[0] // sum(loads)))
    least = 1 if total - largest >= number_of - 1 else 0
    holding, rest = [largest] + [least] * (number_of - 1), total - largest - least * (number_of - 1)
    while rest > 0:
        free = [i for i in range(1, number_of) if holding[i] < largest] or [i for i in range(1, number_of) if holding[i] < limit]
        mass, remaining = sum([loads[i] for i in free]), rest
        for i in free:
            extra = min(limit - holding[i], max(1, remaining * loads[i] // mass), rest)
            holding[i] = holding[i] + extra
            rest = rest - extra
    return np.array(holding)


def centred(key, shape, spread, reach, shards=(), held_as=jnp.bfloat16):
    values = spread * jax.random.normal(key, shape, jnp.float32)
    if shards:
        values = values * shard_levels(key, shape, shards, -0.22, 0.18)
    return jnp.clip(values, -reach, reach).astype(held_as)


def setup_inputs(seed: int = 0) -> dict:
    streams_of = jax.random.split(jax.random.key(seed), 15)
    tokens = centred(streams_of[0], (TOKENS, D), 1.0, 6.0, ((0, 32),))
    gain_attn = jnp.clip(1.0 + 0.1 * jax.random.normal(streams_of[1], (D,), jnp.float32), 0.5, 1.5).astype(jnp.bfloat16)
    w_query = centred(streams_of[2], (D, D), D ** -0.5, 0.21875, ((0, 8),))
    w_key = centred(streams_of[3], (D, D), D ** -0.5, 0.21875, ((0, 8),))
    w_value = centred(streams_of[4], (D, D), D ** -0.5, 0.21875, ((0, 8),))
    w_out = centred(streams_of[5], (D, D), (max(D // 256, 1)) ** -0.5, 3.5, ((0, 8),))
    gain_ffn = jnp.clip(1.0 + 0.1 * jax.random.normal(streams_of[6], (D,), jnp.float32), 0.5, 1.5).astype(jnp.bfloat16)
    w_router = centred(streams_of[7], (D, EXPERTS), 0.025, 0.14941406, ((0, 8),))
    w_in = centred(streams_of[8], (EXPERTS, D, FF), D ** -0.5, 0.21875, ((0, 8),))
    w_expert_out = centred(streams_of[9], (EXPERTS, FF, D), (max(FF // 256, 1)) ** -0.5, 1.75, ((0, 8),))
    bias_table = centred(streams_of[10], (BUCKETS, HEADS), 1.0, 4.0, ((0, 8),))
    bucket_ids = place_ends(jax.random.randint(streams_of[11], (2 * SEQ - 1,), 0, BUCKETS), jax.random.fold_in(streams_of[11], 1), 0, BUCKETS - 1).astype(jnp.int32)
    routes_keys = jax.random.split(jax.random.fold_in(streams_of[12], 1), TOKENS // TOK_DEV)
    routes_turns = jax.random.permutation(jax.random.fold_in(streams_of[12], 3), TOKENS // TOK_DEV)
    routes = jax.vmap(lambda own, number: shared_out(jax.random.fold_in(streams_of[12], 2), own, number, TOK_DEV, EXPERTS, 1, CAP, 1))(routes_keys, routes_turns).reshape((TOKENS, 1))
    cotangent = centred(streams_of[13], (TOKENS, D), 1.0, 6.0, ((0, 32),))
    return dict(tokens=tokens, gain_attn=gain_attn, w_query=w_query, w_key=w_key, w_value=w_value, w_out=w_out, gain_ffn=gain_ffn, w_router=w_router, w_in=w_in, w_expert_out=w_expert_out, bias_table=bias_table, bucket_ids=bucket_ids, routes=routes, cotangent=cotangent)


@jax.custom_vjp
def low(v):
    return lax.optimization_barrier(v.astype(jnp.bfloat16)).astype(jnp.float32)

@jax.custom_vjp
def low_back(v):
    return v

def low_keep(v):
    return (low(v), None)

def low_pass(kept, grad):
    return (grad,)

def back_keep(v):
    return (v, None)

def back_low(kept, grad):
    return (low(grad),)
low.defvjp(low_keep, low_pass)
low_back.defvjp(back_keep, back_low)
EPS = 1e-06
SCALE = 0.125
HIGH = lax.Precision.HIGHEST

def norm_apply(values, gain_vec):
    factor = lax.rsqrt(lax.optimization_barrier(jnp.mean(values * values, axis=-1, keepdims=True)) + EPS)
    return values * factor * gain_vec

def both_round(values):
    return low(low_back(values))

def attend_sequence(query_sequence, key_seq, value_seq, shift_bias):
    block_rows = min(512, SEQ)

    def one_block(block_position):
        row_start = (block_position * block_rows).astype(jnp.int32)
        query_part = lax.dynamic_slice_in_dim(query_sequence, row_start, block_rows, 0)
        bias_part = lax.dynamic_slice_in_dim(shift_bias, row_start, block_rows, 1)
        logits = jnp.einsum('qhd,khd->hqk', query_part, key_seq, precision=HIGH) * SCALE + bias_part
        logits = low_back(logits)
        weights_low = low(jax.nn.softmax(logits, axis=-1))
        return jnp.einsum('hqk,khd->qhd', weights_low, value_seq, precision=HIGH)
    pieces = lax.map(jax.checkpoint(one_block), jnp.arange(SEQ // block_rows, dtype=jnp.int32))
    return pieces.reshape(SEQ, D)

def layer_block(inputs, chosen, gain_one, w_query, w_key, w_value, w_out, gain_two, w_router, w_in, w_expert_out, shift_bias):
    normed = low(norm_apply(inputs, gain_one))
    queries = both_round(jnp.dot(normed, w_query, precision=HIGH)).reshape(SEQS_DEV, SEQ, HEADS, HEAD_DIM)
    keys_all = both_round(jnp.dot(normed, w_key, precision=HIGH)).reshape(SEQS_DEV, SEQ, HEADS, HEAD_DIM)
    values_all = both_round(jnp.dot(normed, w_value, precision=HIGH)).reshape(SEQS_DEV, SEQ, HEADS, HEAD_DIM)
    attended = [attend_sequence(queries[seq_index], keys_all[seq_index], values_all[seq_index], shift_bias) for seq_index in range(SEQS_DEV)]
    mixed = both_round(jnp.concatenate(attended, axis=0))
    middle = inputs + low_back(jnp.dot(mixed, w_out, precision=HIGH))
    routed_in = low(norm_apply(middle, gain_two))
    router_probs = jax.nn.softmax(jnp.dot(routed_in, w_router, precision=HIGH), axis=-1)
    picked = chosen[:, None] == jnp.arange(EXPERTS, dtype=jnp.int32)[None, :]
    gate_value = lax.optimization_barrier(jnp.sum(jnp.where(picked, router_probs, jnp.zeros_like(router_probs)), axis=1))
    running = jnp.cumsum(picked.astype(jnp.int32), axis=0)
    slot_index = (lax.optimization_barrier(jnp.sum(running * picked.astype(jnp.int32), axis=1)) - 1).astype(jnp.int32)
    buffer_in = jnp.zeros((EXPERTS, CAP, D), jnp.float32).at[chosen, slot_index].set(low_back(routed_in))
    hidden_pre = low_back(jnp.einsum('ecd,edf->ecf', buffer_in, w_in, precision=HIGH))
    hidden_act = low(jax.nn.gelu(hidden_pre, approximate=False))
    expert_result = both_round(jnp.einsum('ecf,efd->ecd', hidden_act, w_expert_out, precision=HIGH))
    branch_out = expert_result[chosen, slot_index]
    return middle + gate_value[:, None] * branch_out

def forward(tokens, gain_one, w_query, w_key, w_value, w_out, gain_two, w_router, w_in, w_expert_out, bias_table, bucket_ids, routes):
    position = jnp.arange(SEQ, dtype=jnp.int32)
    shift = position[None, :] - position[:, None] + (SEQ - 1)
    shift_bias = jnp.transpose(bias_table[bucket_ids[shift]], (2, 0, 1))
    token_blocks = tokens.reshape(-1, TOK_DEV, D)
    route_blocks = routes.reshape(-1, TOK_DEV).astype(jnp.int32)
    checked = jax.checkpoint(layer_block)

    def scan_step(unused, member):
        result = checked(member[0], member[1], gain_one, w_query, w_key, w_value, w_out, gain_two, w_router, w_in, w_expert_out, shift_bias)
        return (unused, result)
    _, outputs = lax.scan(scan_step, jnp.zeros((), jnp.float32), (token_blocks, route_blocks))
    return outputs.reshape(-1, D)

def reference(tokens, gain_attn, w_query, w_key, w_value, w_out, gain_ffn, w_router, w_in, w_expert_out, bias_table, bucket_ids, routes, cotangent):
    as_floats = tuple((member.astype(jnp.float32) for member in (tokens, gain_attn, w_query, w_key, w_value, w_out, gain_ffn, w_router, w_in, w_expert_out, bias_table)))

    def apply_all(*params):
        return forward(*params, bucket_ids, routes)
    output, pullback = jax.vjp(apply_all, *as_floats)
    gradients = pullback(cotangent.astype(jnp.float32))
    return (output.astype(jnp.bfloat16), gradients[0], gradients[1], gradients[2], gradients[3], gradients[4], gradients[5], gradients[6], gradients[7], gradients[8], gradients[9], gradients[10])
```

```python
import functools

import jax
import jax.numpy as jnp
from jax import lax
from jax.experimental import pallas as pl
from jax.experimental.pallas import tpu as pltpu
from jax.sharding import PartitionSpec as P

EPS = 1e-06
SCALE = 0.125
HIGH = lax.Precision.HIGHEST
TILE = 256
PAIR = 128
VMEM_BYTES = 56 * 1024 * 1024


def norm_apply(values, gain_vec):
    factor = lax.rsqrt(jnp.mean(values * values, axis=-1, keepdims=True) + EPS)
    return values * factor * gain_vec


def inner_rows(first_op, second_op):
    return lax.dot_general(
        first_op, second_op, (((0,), (0,)), ((), ())), preferred_element_type=jnp.float32
    )


def by_rows(first_op, second_op):
    return lax.dot_general(
        first_op, second_op, (((1,), (1,)), ((), ())), preferred_element_type=jnp.float32
    )


def plain(first_op, second_op):
    return jnp.dot(first_op, second_op, preferred_element_type=jnp.float32)


def flipped(block):
    return block.astype(jnp.float32).T.astype(block.dtype)


def fill_bias(rev_ref, bias_ref, tiles):
    span = rev_ref.shape[-1]
    for a in range(2):
        wide = jnp.broadcast_to(rev_ref[0, a : a + 1, :], (TILE, span))
        wide = pltpu.roll(wide, span - (TILE - 1), 1, stride=1, stride_axis=0)
        for t in range(2 * tiles - 1):
            bias_ref[a, t] = wide[:, t * TILE : (t + 1) * TILE]


def head_mask(rows, a):
    lane = lax.broadcasted_iota(jnp.int32, (rows, PAIR), 1)
    return (lane < PAIR // 2) if a == 0 else (lane >= PAIR // 2)


def keep_head(block, a):
    wide = block.astype(jnp.float32)
    return jnp.where(head_mask(block.shape[0], a), wide, 0.0)


def attend_kernel(tiles, q_ref, k_ref, v_ref, rev_ref, mixed_ref, lse_ref, bias_ref, vt_ref):
    step = pl.program_id(1)

    @pl.when(step == 0)
    def _():
        fill_bias(rev_ref, bias_ref, tiles)
        vt_ref[...] = flipped(v_ref[...])

    half = PAIR // 2
    outs = []
    for a in range(2):
        q_one = (keep_head(q_ref[...], a) * SCALE).astype(jnp.bfloat16)
        parts = []
        top = None
        for kb in range(tiles):
            part = by_rows(k_ref[kb * TILE : (kb + 1) * TILE, :], q_one)
            part = part + bias_ref[a, step - kb + tiles - 1]
            parts.append(part)
            high = jnp.max(part, axis=0, keepdims=True)
            top = high if top is None else jnp.maximum(top, high)
        total = jnp.zeros_like(top)
        exps = []
        for kb in range(tiles):
            part = jnp.exp(parts[kb] - top)
            total = total + jnp.sum(part, axis=0, keepdims=True)
            exps.append(part)
        scale = 1.0 / total
        out = jnp.zeros((half, TILE), jnp.float32)
        for kb in range(tiles):
            low = (exps[kb] * scale).astype(jnp.bfloat16)
            out = out + plain(
                vt_ref[a * half : (a + 1) * half, kb * TILE : (kb + 1) * TILE], low
            )
        outs.append(out)
        lse_ref[0, a : a + 1, :] = top + jnp.log(total)
    mixed_ref[...] = jnp.concatenate(outs, axis=0).T.astype(jnp.bfloat16)


def back_kernel(
    tiles, q_ref, k_ref, v_ref, grad_ref, mixed_ref, lse_ref, rev_ref,
    dq_ref, dk_ref, dv_ref, diag_ref,
    bias_ref, kt_ref, fold_ref, dk_sum, dv_sum,
):
    step = pl.program_id(1)

    @pl.when(step == 0)
    def _():
        fill_bias(rev_ref, bias_ref, tiles)
        kt_ref[...] = flipped(k_ref[...])
        fold_ref[...] = jnp.zeros_like(fold_ref)
        dk_sum[...] = jnp.zeros_like(dk_sum)
        dv_sum[...] = jnp.zeros_like(dv_sum)

    half = PAIR // 2
    along = (grad_ref[...].astype(jnp.float32) * mixed_ref[...].astype(jnp.float32)).T
    outs = []
    for a in range(2):
        q_one = (keep_head(q_ref[...], a) * SCALE).astype(jnp.bfloat16)
        grad_one = keep_head(grad_ref[...], a).astype(jnp.bfloat16)
        shared = jnp.sum(along[a * half : (a + 1) * half], axis=0, keepdims=True)
        lse = lse_ref[0, a : a + 1, :]
        out = jnp.zeros((half, TILE), jnp.float32)
        for kb in range(tiles):
            rows = slice(kb * TILE, (kb + 1) * TILE)
            spot = step - kb + tiles - 1
            score = by_rows(k_ref[rows, :], q_one) + bias_ref[a, spot]
            prob = jnp.exp(score - lse)
            prob_grad = by_rows(v_ref[rows, :], grad_one)
            score_grad = prob * (prob_grad - shared)
            fold_ref[a, spot] += score_grad
            low = score_grad.astype(jnp.bfloat16)
            dv_sum[rows, :] += plain(prob.astype(jnp.bfloat16), grad_one)
            dk_sum[rows, :] += plain(low, q_one)
            out = out + plain(kt_ref[a * half : (a + 1) * half, rows], low)
        outs.append(out * SCALE)
    dq_ref[...] = jnp.concatenate(outs, axis=0).T.astype(jnp.bfloat16)

    @pl.when(step == tiles - 1)
    def _():
        dk_ref[...] = dk_sum[...].astype(jnp.bfloat16)
        dv_ref[...] = dv_sum[...].astype(jnp.bfloat16)
        for a in range(2):
            wide = jnp.concatenate(
                [fold_ref[a, t] for t in range(2 * tiles - 1)]
                + [jnp.zeros((TILE, TILE), jnp.float32)],
                axis=1,
            )
            rows = TILE
            while rows > 8:
                rows //= 2
                wide = pltpu.roll(wide[:rows], rows, 1) + wide[rows:]
            place = lax.broadcasted_iota(jnp.int32, wide.shape, 0)
            for bit in (4, 2, 1):
                wide = jnp.where((place & bit) == 0, pltpu.roll(wide, bit, 1), wide)
            diag_ref[0, a : a + 1, :] = jnp.sum(wide, axis=0, keepdims=True)


def attend_forward(qkv, rev):
    seq_len = qkv.shape[0]
    width = qkv.shape[1] // 3
    pairs, tiles = width // PAIR, seq_len // TILE
    span = rev.shape[-1]
    return pl.pallas_call(
        functools.partial(attend_kernel, tiles),
        grid=(pairs, tiles),
        in_specs=[
            pl.BlockSpec((TILE, PAIR), lambda p, s: (s, p)),
            pl.BlockSpec((seq_len, PAIR), lambda p, s: (0, pairs + p)),
            pl.BlockSpec((seq_len, PAIR), lambda p, s: (0, 2 * pairs + p)),
            pl.BlockSpec((1, 2, span), lambda p, s: (p, 0, 0)),
        ],
        out_specs=[
            pl.BlockSpec((TILE, PAIR), lambda p, s: (s, p)),
            pl.BlockSpec((1, 2, TILE), lambda p, s: (p, 0, s)),
        ],
        out_shape=[
            jax.ShapeDtypeStruct((seq_len, width), jnp.bfloat16),
            jax.ShapeDtypeStruct((pairs, 2, seq_len), jnp.float32),
        ],
        scratch_shapes=[
            pltpu.VMEM((2, 2 * tiles - 1, TILE, TILE), jnp.float32),
            pltpu.VMEM((PAIR, seq_len), jnp.bfloat16),
        ],
        compiler_params=pltpu.CompilerParams(vmem_limit_bytes=VMEM_BYTES),
        cost_estimate=pl.CostEstimate(
            flops=16 * seq_len * seq_len * width,
            bytes_accessed=8 * seq_len * width,
            transcendentals=seq_len * seq_len * 2 * pairs,
        ),
    )(qkv, qkv, qkv, rev)


def attend_backward(qkv, mixed_grad, mixed, lse, rev):
    seq_len, width = mixed.shape
    pairs, tiles = width // PAIR, seq_len // TILE
    span = rev.shape[-1]
    row_spec = pl.BlockSpec((TILE, PAIR), lambda p, s: (s, p))
    full = jax.ShapeDtypeStruct((seq_len, width), jnp.bfloat16)
    return pl.pallas_call(
        functools.partial(back_kernel, tiles),
        grid=(pairs, tiles),
        in_specs=[
            row_spec,
            pl.BlockSpec((seq_len, PAIR), lambda p, s: (0, pairs + p)),
            pl.BlockSpec((seq_len, PAIR), lambda p, s: (0, 2 * pairs + p)),
            row_spec,
            row_spec,
            pl.BlockSpec((1, 2, TILE), lambda p, s: (p, 0, s)),
            pl.BlockSpec((1, 2, span), lambda p, s: (p, 0, 0)),
        ],
        out_specs=[
            row_spec,
            pl.BlockSpec((seq_len, PAIR), lambda p, s: (0, p)),
            pl.BlockSpec((seq_len, PAIR), lambda p, s: (0, p)),
            pl.BlockSpec((1, 2, span), lambda p, s: (p, 0, 0)),
        ],
        out_shape=[full, full, full, jax.ShapeDtypeStruct((pairs, 2, span), jnp.float32)],
        scratch_shapes=[
            pltpu.VMEM((2, 2 * tiles - 1, TILE, TILE), jnp.float32),
            pltpu.VMEM((PAIR, seq_len), jnp.bfloat16),
            pltpu.VMEM((2, 2 * tiles - 1, TILE, TILE), jnp.float32),
            pltpu.VMEM((seq_len, PAIR), jnp.float32),
            pltpu.VMEM((seq_len, PAIR), jnp.float32),
        ],
        compiler_params=pltpu.CompilerParams(vmem_limit_bytes=VMEM_BYTES),
        cost_estimate=pl.CostEstimate(
            flops=seq_len * width, bytes_accessed=16 * seq_len * width, transcendentals=0
        ),
    )(qkv, qkv, qkv, mixed_grad, mixed, lse, rev)


def expert_kernel(
    rows_ref, win_ref, wout_ref, back_ref, gin_ref, gout_ref, flip_ref, result_sum, rows_sum
):
    step = pl.program_id(0)
    width = win_ref.shape[0]
    count = rows_ref.shape[0]
    chunk = count // 3

    @pl.when(step == 0)
    def _():
        for c in range(3):
            rows = slice(c * chunk, (c + 1) * chunk)
            flip_ref[:, rows] = flipped(rows_ref[rows, :width])
        result_sum[...] = jnp.zeros_like(result_sum)
        rows_sum[...] = jnp.zeros_like(rows_sum)

    grad_in = jnp.zeros(gin_ref.shape, jnp.float32)
    grad_out = jnp.zeros(gout_ref.shape, jnp.float32)
    for c in range(3):
        rows = slice(c * chunk, (c + 1) * chunk)
        given = rows_ref[rows, :width]
        upstream = rows_ref[rows, width:]
        pre = plain(given, win_ref[...])
        cdf = 0.5 + 0.5 * lax.erf(pre * 0.7071067811865476)
        slope = cdf + pre * (jnp.exp(-0.5 * pre * pre) * 0.3989422804014327)
        act = pre * cdf
        act_low = act.astype(jnp.bfloat16)
        result_sum[rows, :] += plain(act_low, wout_ref[...])
        pre_grad = (by_rows(upstream, wout_ref[...]) * slope).astype(jnp.bfloat16)
        rows_sum[rows, :] += by_rows(pre_grad, win_ref[...])
        grad_in = grad_in + plain(flip_ref[:, rows], pre_grad)
        grad_out = grad_out + plain(act.T.astype(jnp.bfloat16), upstream)
    gin_ref[...] = grad_in.astype(jnp.bfloat16)
    gout_ref[...] = grad_out.astype(jnp.bfloat16)

    @pl.when(step == pl.num_programs(0) - 1)
    def _():
        back_ref[:, :width] = result_sum[...].astype(jnp.bfloat16)
        back_ref[:, width:] = rows_sum[...].astype(jnp.bfloat16)


def run_expert(rows, w_in, w_expert_out):
    count = rows.shape[0]
    width, hidden = w_in.shape
    return pl.pallas_call(
        expert_kernel,
        grid=(hidden // TILE,),
        in_specs=[
            pl.BlockSpec((count, 2 * width), lambda f: (0, 0)),
            pl.BlockSpec((width, TILE), lambda f: (0, f)),
            pl.BlockSpec((TILE, width), lambda f: (f, 0)),
        ],
        out_specs=[
            pl.BlockSpec((count, 2 * width), lambda f: (0, 0)),
            pl.BlockSpec((width, TILE), lambda f: (0, f)),
            pl.BlockSpec((TILE, width), lambda f: (f, 0)),
        ],
        out_shape=[
            jax.ShapeDtypeStruct((count, 2 * width), jnp.bfloat16),
            jax.ShapeDtypeStruct((width, hidden), jnp.bfloat16),
            jax.ShapeDtypeStruct((hidden, width), jnp.bfloat16),
        ],
        scratch_shapes=[
            pltpu.VMEM((width, count), jnp.bfloat16),
            pltpu.VMEM((count, width), jnp.float32),
            pltpu.VMEM((count, width), jnp.float32),
        ],
        compiler_params=pltpu.CompilerParams(vmem_limit_bytes=VMEM_BYTES),
        cost_estimate=pl.CostEstimate(
            flops=12 * count * width * hidden,
            bytes_accessed=8 * count * width + 8 * width * hidden,
            transcendentals=2 * count * hidden,
        ),
    )(rows, w_in, w_expert_out)


def pad_rows(column, rows):
    return jnp.pad(column, (0, rows - column.shape[0]))[:, None]


def sum_replicas(share):
    count = lax.axis_size("rep")
    here = lax.axis_index("rep")
    held = [share]
    for shift in range(1, count):
        route = [(source, (source + shift) % count) for source in range(count)]
        held.append(lax.ppermute(share, "rep", route))
    total = jnp.zeros(share.shape, jnp.float32)
    for owner in range(count):
        behind = lax.rem(here - owner + count, count)
        piece = held[0].astype(jnp.float32)
        for shift in range(1, count):
            piece = jnp.where(behind == shift, held[shift].astype(jnp.float32), piece)
        total = total + piece
    return total


def shards(
    tokens, gain_attn, w_query, w_key, w_value, w_out, gain_ffn, w_router, w_in, w_expert_out,
    bias_table, bucket_ids, routes, cotangent,
):
    low = jnp.bfloat16
    row_count, width = tokens.shape
    part = w_query.shape[0]
    group = width // part
    table_rows, heads = bias_table.shape
    buckets = table_rows * group
    experts = w_router.shape[1]
    used = experts + 3
    filler = -used % PAIR
    packed = jnp.concatenate(
        [
            w_query, w_key, w_value, w_out, w_router, gain_attn[:, None], gain_ffn[:, None],
            pad_rows(bias_table.reshape(-1), part), jnp.zeros((part, filler), low),
        ],
        axis=1,
    )
    whole = lax.all_gather(packed, "grp", axis=0, tiled=True)
    qkv_full = whole[:, : 3 * width]
    out_full = whole[:, 3 * width : 4 * width]
    extra = whole[:, 4 * width :]
    router32 = extra[:, :experts].astype(jnp.float32)
    gain_one32 = extra[:, experts].astype(jnp.float32)
    gain_two32 = extra[:, experts + 1].astype(jnp.float32)
    table_full = (
        extra[:, experts + 2].reshape(group, part)[:, : table_rows * heads].reshape(buckets, heads)
    )
    seq_len = (bucket_ids.shape[0] + 1) // 2
    capacity = 3 * row_count // (2 * experts)

    rev_ids = jnp.pad(bucket_ids[::-1], (0, 1), constant_values=buckets)
    select = (rev_ids[:, None] == jnp.arange(buckets, dtype=jnp.int32)[None, :]).astype(
        jnp.float32
    )
    rev = lax.dot_general(
        table_full.astype(jnp.float32), select, (((0,), (1,)), ((), ())), precision=HIGH
    ).reshape(heads // 2, 2, 2 * seq_len)

    chosen = routes[:, 0]
    picked = chosen[:, None] == jnp.arange(experts, dtype=jnp.int32)[None, :]
    picked_float = picked.astype(jnp.float32)
    place = jnp.arange(row_count, dtype=jnp.int32)
    before = (place[None, :] < place[:, None]).astype(low)
    running = plain(before, picked.astype(low))
    slot = jnp.sum(running * picked_float, axis=1).astype(jnp.int32)
    target = chosen * capacity + slot

    inputs = tokens.astype(jnp.float32)
    upstream = cotangent.astype(jnp.float32)
    normed = norm_apply(inputs, gain_one32).astype(low)
    qkv = plain(normed, qkv_full).astype(low)
    mixed, lse = attend_forward(qkv, rev)
    middle = inputs + plain(mixed, out_full)
    routed_in = norm_apply(middle, gain_two32).astype(low)
    router_logits = jnp.dot(routed_in.astype(jnp.float32), router32, precision=HIGH)
    router_probs = jax.nn.softmax(router_logits, axis=-1)
    gate_value = jnp.sum(router_probs * picked_float, axis=1)
    result_grad = (upstream * gate_value[:, None]).astype(low)

    slots = jnp.arange(experts * capacity, dtype=jnp.int32)
    spread = (slots[:, None] == target[None, :]).astype(low)
    together = jnp.concatenate([routed_in, result_grad], axis=1)
    sent = plain(spread, together).astype(low)
    arrived = lax.all_to_all(sent, "grp", split_axis=0, concat_axis=0, tiled=True)
    answer, grad_in_low, grad_out_low = run_expert(arrived, w_in[0], w_expert_out[0])
    grad_in_low, grad_out_low = lax.psum((grad_in_low, grad_out_low), "rep")
    back = lax.all_to_all(answer, "grp", split_axis=0, concat_axis=0, tiled=True)
    collect = (target[:, None] == slots[None, :]).astype(low)
    returned = plain(collect, back)
    branch_out = returned[:, :width]
    expert_part = returned[:, width:]
    output = (middle + gate_value[:, None] * branch_out).astype(low)

    gate_grad = jnp.sum(upstream * branch_out, axis=1)
    logit_grad = router_probs * (
        picked_float * gate_grad[:, None] - (gate_value * gate_grad)[:, None]
    )
    grad_router = lax.dot_general(
        routed_in.astype(jnp.float32), logit_grad, (((0,), (0,)), ((), ())), precision=HIGH
    )
    routed_grad = expert_part + lax.dot_general(
        logit_grad, router32, (((1,), (1,)), ((), ())), precision=HIGH
    )
    _, second_pull = jax.vjp(norm_apply, middle, gain_two32)
    middle_section, grad_gain_ffn = second_pull(routed_grad)
    middle_grad = upstream + middle_section
    out_low = middle_grad.astype(low)
    mixed_grad = by_rows(out_low, out_full).astype(low)
    query_grad, key_grad, value_grad, diagonals = attend_backward(qkv, mixed_grad, mixed, lse, rev)
    grad_table = lax.dot_general(
        select, diagonals.reshape(heads, 2 * seq_len), (((0,), (1,)), ((), ())), precision=HIGH
    )
    normed_grad = (
        by_rows(query_grad, qkv_full[:, :width])
        + by_rows(key_grad, qkv_full[:, width : 2 * width])
        + by_rows(value_grad, qkv_full[:, 2 * width :])
    )
    _, first_pull = jax.vjp(norm_apply, inputs, gain_one32)
    input_part, grad_gain_attn = first_pull(normed_grad)
    input_grad = middle_grad + input_part
    table_column = jnp.pad(
        grad_table.reshape(group, table_rows * heads), ((0, 0), (0, part - table_rows * heads))
    ).reshape(width, 1)
    extra_grad = jnp.concatenate(
        [
            grad_router.astype(low),
            grad_gain_attn[:, None].astype(low),
            grad_gain_ffn[:, None].astype(low),
            table_column.astype(low),
            jnp.zeros((width, filler), low),
        ],
        axis=1,
    )
    pieces = lax.optimization_barrier(
        (
            inner_rows(normed, query_grad).astype(low),
            inner_rows(normed, key_grad).astype(low),
            inner_rows(normed, value_grad).astype(low),
            inner_rows(mixed, out_low).astype(low),
            extra_grad,
        )
    )
    swapped = lax.all_to_all(
        jnp.concatenate(pieces, axis=1), "grp", split_axis=0, concat_axis=0, tiled=True
    )
    share = jnp.sum(swapped.reshape(group, part, -1).astype(jnp.float32), axis=0).astype(low)
    mine = sum_replicas(share)
    small = mine[:, 4 * width :]
    return (
        output,
        input_grad,
        small[:, experts],
        mine[:, :width],
        mine[:, width : 2 * width],
        mine[:, 2 * width : 3 * width],
        mine[:, 3 * width : 4 * width],
        small[:, experts + 1],
        small[:, :experts],
        grad_in_low.astype(jnp.float32)[None],
        grad_out_low.astype(jnp.float32)[None],
        small[: table_rows * heads, experts + 2].reshape(table_rows, heads),
    )


def solution(mesh):
    rows = P(("grp", "rep"), None)
    split, split_two, split_three = P("grp"), P("grp", None), P("grp", None, None)
    in_specs = (
        rows, split, split_two, split_two, split_two, split_two, split, split_two,
        split_three, split_three, split_two, P(), rows, rows,
    )
    out_specs = (
        rows, rows, split, split_two, split_two, split_two, split_two, split, split_two,
        split_three, split_three, split_two,
    )
    return jax.shard_map(shards, mesh=mesh, in_specs=in_specs, out_specs=out_specs, check_vma=False)
```
